768 devices in a mesh: ctx: 12 (over z), head: 64 (over x, y, core).
Axes of the slice: x: 4, y: 8, z: 12, core: 2. Of those that a mesh axis runs over, the one named last changes fastest.
Arguments:
- queries: bfloat16 [8, 8, 12, 64, 12, 256], P(None, None, 'ctx', 'head'), may hold values from -6 to 6
- keys: bfloat16 [8, 8, 12, 64, 12, 256], P(None, None, 'ctx', 'head'), may hold values from -6 to 6
- values: bfloat16 [8, 8, 12, 64, 12, 256], P(None, None, 'ctx', 'head'), may hold values from -6 to 6
- gates: bfloat16 [8, 8, 12, 64, 12, 256], P(None, None, 'ctx', 'head'), may hold values from -6 to 6
- out_grad: bfloat16 [8, 8, 12, 64, 12, 256], P(None, None, 'ctx', 'head'), may hold values from -6 to 6
- gains: float32 [8, 256], replicated, may hold values from 0.5 to 1.5
Outputs:
- grad_queries: bfloat16 [8, 8, 12, 64, 12, 256], P(None, None, 'ctx', 'head')
- grad_keys: bfloat16 [8, 8, 12, 64, 12, 256], P(None, None, 'ctx', 'head')
- grad_values: bfloat16 [8, 8, 12, 64, 12, 256], P(None, None, 'ctx', 'head')
The draws below stay inside these ranges and needn't reach their ends.
All inputs are finite; a program needn't handle non-finite values.
Results may differ from the reference program's by a relative error of at most 0.007.
Values may be sent and summed in bfloat16 or wider, within the bound.
No kernel may reach another device: no remote copies, remote signals or barrier semaphores. Data moves between devices by JAX's collectives and lax.ppermute only.
A program may use at most 64 MiB of HBM per device.

```python
import jax
import jax.numpy as jnp
from jax import lax

HEADS = 8
DH = 256
TOK_DEV = 768
SPLIT = 8
PIECE = 12
N_CTX = 12
N_HEAD = 64


def levels(own_key, dims, cuts, least, high):
    def one(dim, blocks):
        draws = jax.random.uniform(jax.random.fold_in(jax.random.fold_in(own_key, 6), dim), (blocks,), jnp.float32, least / len(cuts), high / len(cuts))
        return jnp.repeat(jnp.exp(draws), dims[dim] // blocks).reshape((-1,) + (1,) * (len(dims) - dim - 1))

    level = one(*cuts[0])
    for cut in cuts[1:]:
        level = level * one(*cut)
    return level


def bell_draw(key, shape, scale, most, split=(), kind=jnp.bfloat16):
    factor_of = levels(key, shape, split, -0.22, 0.18) if split else 1.0
    result = jax.random.normal(key, shape, jnp.float32) * scale * factor_of
    return jnp.minimum(jnp.maximum(result, -most), most).astype(kind)


def setup_inputs(seed: int = 0) -> dict:
    splits = jax.random.split(jax.random.key(seed), 7)
    return {
        "queries": bell_draw(splits[0], (SPLIT, HEADS, N_CTX, N_HEAD, PIECE, DH), 1.0, 6.0, ((2, 12), (3, 64))),
        "keys": bell_draw(splits[1], (SPLIT, HEADS, N_CTX, N_HEAD, PIECE, DH), 1.0, 6.0, ((2, 12), (3, 64))),
        "values": bell_draw(splits[2], (SPLIT, HEADS, N_CTX, N_HEAD, PIECE, DH), 1.0, 6.0, ((2, 12), (3, 64))),
        "gates": bell_draw(splits[3], (SPLIT, HEADS, N_CTX, N_HEAD, PIECE, DH), 1.5, 6.0, ((2, 12), (3, 64))),
        "out_grad": bell_draw(splits[4], (SPLIT, HEADS, N_CTX, N_HEAD, PIECE, DH), 1.0, 6.0, ((2, 12), (3, 64))),
        "gains": jnp.clip(jax.random.uniform(splits[5], (HEADS, DH), jnp.float32, 0.5, 1.5), 0.5, 1.5),
    }


HIGH = lax.Precision.HIGHEST

def one_problem(items):
    q, k, v, g, d, gain = items
    f32 = jnp.float32
    qf = q.astype(f32)
    kf = k.astype(f32)
    vf = v.astype(f32)
    rows = q.shape[1]
    causal = jnp.arange(rows)[:, None] >= jnp.arange(rows)[None, :]
    state = jnp.einsum('cse,csf->cef', kf, vf, precision=HIGH)
    zero = jnp.zeros((1,) + state.shape[1:], f32)
    carried = jnp.concatenate([zero, jnp.cumsum(state, 0)[:-1]], 0).astype(jnp.bfloat16).astype(f32)
    scores = jnp.einsum('cte,cse->cts', qf, kf, precision=HIGH)
    masked = jnp.where(causal[None], scores, 0.0).astype(jnp.bfloat16).astype(f32)
    mixed = jnp.einsum('cte,cef->ctf', qf, carried, precision=HIGH) + jnp.einsum('cts,csf->ctf', masked, vf, precision=HIGH)
    inv = lax.rsqrt(lax.optimization_barrier(jnp.mean(mixed * mixed, -1, keepdims=True)) + 1e-05)
    normed = mixed * inv
    dnormed = d.astype(f32) * gain[None, None, :] * jax.nn.silu(g.astype(f32))
    dmixed = inv * (dnormed - normed * lax.optimization_barrier(jnp.mean(dnormed * normed, -1, keepdims=True)))
    dmixed = dmixed.astype(jnp.bfloat16).astype(f32)
    back_state = jnp.einsum('cte,ctf->cef', qf, dmixed, precision=HIGH)
    reversed_sum = jnp.cumsum(back_state[::-1], 0)[::-1]
    later = jnp.concatenate([reversed_sum[1:], zero], 0).astype(jnp.bfloat16).astype(f32)
    across = jnp.einsum('ctf,csf->cts', dmixed, vf, precision=HIGH)
    across = jnp.where(causal[None], across, 0.0).astype(jnp.bfloat16).astype(f32)
    grad_q = jnp.einsum('ctf,cef->cte', dmixed, carried, precision=HIGH) + jnp.einsum('cts,cse->cte', across, kf, precision=HIGH)
    grad_k = jnp.einsum('csf,cef->cse', vf, later, precision=HIGH) + jnp.einsum('cts,cte->cse', across, qf, precision=HIGH)
    grad_v = jnp.einsum('cse,cef->csf', kf, later, precision=HIGH) + jnp.einsum('cts,ctf->csf', masked, dmixed, precision=HIGH)
    return (grad_q.astype(jnp.bfloat16), grad_k.astype(jnp.bfloat16), grad_v.astype(jnp.bfloat16))

def reference(queries, keys, values, gates, out_grad, gains):
    shape = queries.shape
    heads = shape[1]
    inner = shape[5]
    blocks = shape[0] * shape[2]

    def flat(x):
        return jnp.swapaxes(x, 0, 1).reshape((heads, blocks, TOK_DEV, inner))

    def unflat(x):
        return jnp.swapaxes(x.reshape((heads, shape[0]) + shape[2:]), 0, 1)
    grad_q, grad_k, grad_v = lax.map(one_problem, (flat(queries), flat(keys), flat(values), flat(gates), flat(out_grad), gains.astype(jnp.float32)))
    return (unflat(grad_q), unflat(grad_k), unflat(grad_v))
```

```python
import jax
import jax.numpy as jnp
from jax import lax
from jax.experimental import pallas as pl
from jax.experimental.pallas import tpu as pltpu
from jax.sharding import PartitionSpec as P

F32 = jnp.float32
BF16 = jnp.bfloat16


def exchange(x, axes, groups=None):
    return lax.all_to_all(x, axes, 0, 0, axis_index_groups=groups, tiled=True)


def scan_kernel(reverse, blocks, in_ref, out_ref):
    running = jnp.zeros(in_ref.shape[1:], F32)
    for position in range(blocks):
        block = blocks - 1 - position if reverse else position
        out_ref[block] = running.astype(BF16)
        running = running + in_ref[block].astype(F32)


def exclusive_sum(pieces, reverse):
    blocks = pieces.shape[0]

    def body(in_ref, out_ref):
        scan_kernel(reverse, blocks, in_ref, out_ref)

    return pl.pallas_call(
        body,
        out_shape=jax.ShapeDtypeStruct(pieces.shape, BF16),
        in_specs=[pl.BlockSpec(memory_space=pltpu.VMEM)],
        out_specs=pl.BlockSpec(memory_space=pltpu.VMEM),
    )(pieces)


def carry_states(state, reverse, groups):
    rows, cols = state.shape
    tiles = state.astype(BF16).reshape(rows // 8, 8, cols // 128, 128).transpose(0, 2, 1, 3)
    tiles = jnp.pad(tiles, ((0, 0), (0, 1), (0, 0), (0, 0))).reshape(96, 8, 128)
    gathered = exchange(tiles, ("ctx", "head"), groups)
    summed = exclusive_sum(gathered, reverse)
    back = exchange(summed, ("ctx", "head"), groups).reshape(rows // 8, 3, 8, 128)
    return back[:, :2].transpose(0, 2, 1, 3).reshape(rows, cols)


def local(queries, keys, values, gates, out_grad, gains):
    split, heads, _, _, piece, dh = queries.shape
    shape = queries.shape
    n_ctx = lax.axis_size("ctx")
    n_head = lax.axis_size("head")
    xs, cores = n_head // (heads * 2), 2
    groups = [
        [c * n_head + ((p // 2) * heads + h) * 2 + p % 2 for p in range(split) for c in range(n_ctx)]
        for h in range(heads)
    ]

    def to_pieces(array):
        return array.reshape(xs, cores, heads, piece, dh).transpose(0, 2, 1, 3, 4).reshape(n_head, piece, dh)

    gate = gates.astype(F32)
    dnorm = out_grad.astype(F32) * gains[None, :, None, None, None, :] * jax.nn.silu(gate)
    sent = jnp.concatenate(
        [to_pieces(queries), to_pieces(keys), to_pieces(values), to_pieces(dnorm.astype(BF16))], axis=1
    )
    got = exchange(sent, "head")
    q, k, v, d = (got[:, n * piece : (n + 1) * piece].reshape(n_head * piece, dh) for n in range(4))
    rows = q.shape[0]
    causal = jnp.arange(rows)[:, None] >= jnp.arange(rows)[None, :]
    state = jnp.einsum("se,sf->ef", k, v, preferred_element_type=F32)
    carried = carry_states(state, False, groups)
    scores = jnp.einsum("te,se->ts", q, k, preferred_element_type=F32)
    masked = jnp.where(causal, scores, 0.0).astype(BF16)
    mixed = jnp.dot(q, carried, preferred_element_type=F32) + jnp.dot(masked, v, preferred_element_type=F32)
    inv = lax.rsqrt(jnp.mean(mixed * mixed, -1, keepdims=True) + 1e-05)
    normed = mixed * inv
    dnormed = d.astype(F32)
    dmixed = (inv * (dnormed - normed * jnp.mean(dnormed * normed, -1, keepdims=True))).astype(BF16)
    back_state = jnp.einsum("te,tf->ef", q, dmixed, preferred_element_type=F32)
    later = carry_states(back_state, True, groups)
    across = jnp.einsum("tf,sf->ts", dmixed, v, preferred_element_type=F32)
    across = jnp.where(causal, across, 0.0).astype(BF16)
    grad_q = jnp.einsum("tf,ef->te", dmixed, carried, preferred_element_type=F32) + jnp.dot(
        across, k, preferred_element_type=F32
    )
    grad_k = jnp.einsum("sf,ef->se", v, later, preferred_element_type=F32) + jnp.einsum(
        "ts,te->se", across, q, preferred_element_type=F32
    )
    grad_v = jnp.dot(k, later, preferred_element_type=F32) + jnp.einsum(
        "ts,tf->sf", masked, dmixed, preferred_element_type=F32
    )
    grads = jnp.concatenate([g.astype(BF16).reshape(n_head, piece, dh) for g in (grad_q, grad_k, grad_v)], axis=1)
    back = exchange(grads, "head").reshape(xs, heads, cores, 3 * piece, dh).transpose(0, 2, 1, 3, 4)
    return tuple(back[:, :, :, n * piece : (n + 1) * piece].reshape(shape) for n in range(3))


def solution(mesh):
    placed = P(None, None, "ctx", "head", None, None)
    return jax.shard_map(
        local,
        mesh=mesh,
        in_specs=(placed,) * 5 + (P(),),
        out_specs=(placed,) * 3,
        check_vma=False,
    )
```

```python
import jax
import jax.numpy as jnp
from jax import lax
from jax.sharding import PartitionSpec as P

F32 = jnp.float32
BF16 = jnp.bfloat16


def exchange(x, axes, groups=None):
    return lax.all_to_all(x, axes, 0, 0, axis_index_groups=groups, tiled=True)


def to_pieces(state, n):
    rows, cols = state.shape
    tiles = -(-rows * cols // (8 * 128 * n)) * n
    high = tiles * 128 // cols * 8
    full = jnp.pad(state.astype(BF16), ((0, high - rows), (0, 0)))
    full = full.reshape(high // 8, 8, cols // 128, 128).transpose(0, 2, 1, 3)
    return full.reshape(n, tiles // n, 8, 128).transpose(0, 2, 1, 3).reshape(n, 8, tiles // n * 128)


def from_pieces(pieces, rows, cols):
    n, _, width = pieces.shape
    full = pieces.reshape(n, 8, width // 128, 128).transpose(0, 2, 1, 3)
    full = full.reshape(-1, cols // 128, 8, 128).transpose(0, 2, 1, 3).reshape(-1, cols)
    return full[:rows]


def carry_states(state, rest, meanwhile, reverse, wanted, groups):
    rows, cols = state.shape
    n_ctx = lax.axis_size("ctx")
    split = len(groups[0])
    at = jnp.arange(n_ctx)
    order = (at[:, None] < at[None, :] if reverse else at[:, None] > at[None, :]).astype(BF16)
    pieces, rest = lax.optimization_barrier((to_pieces(state, n_ctx), rest))
    pieces = exchange(pieces, "ctx")
    total = jnp.sum(pieces.astype(F32), 0)
    sent = jnp.broadcast_to(total.astype(BF16)[None], (split,) + total.shape)
    sent, rest = lax.optimization_barrier((sent, rest))
    totals = exchange(sent, "head", groups)
    done = meanwhile(*rest)
    inside = jnp.einsum("ab,brl->arl", order, pieces, preferred_element_type=F32)
    outside = jnp.sum(totals.astype(F32) * wanted[:, None, None], 0)
    back, done = lax.optimization_barrier(((inside + outside[None]).astype(BF16), done))
    back, done = lax.optimization_barrier((exchange(back, "ctx"), done))
    return from_pieces(back, rows, cols), done


def local(queries, keys, values, gates, out_grad, gains):
    split, heads, _, _, piece, dh = queries.shape
    shape = queries.shape
    n_head = lax.axis_size("head")
    xs, cores = n_head // (heads * 2), 2
    groups = [[((p // 2) * heads + h) * 2 + p % 2 for p in range(split)] for h in range(heads)]
    me = lax.axis_index("head")
    row = me // (heads * 2) * 2 + me % 2
    other = jnp.arange(split)
    before, after = ((other < row).astype(F32), (other > row).astype(F32))

    def for_devices(array):
        return array.reshape(xs, cores, heads, piece, dh).transpose(0, 2, 1, 3, 4).reshape(n_head, piece, dh)

    gate = gates.astype(F32)
    dnorm = out_grad.astype(F32) * gains[None, :, None, None, None, :] * jax.nn.silu(gate)
    sent = jnp.concatenate(
        [for_devices(queries), for_devices(keys), for_devices(values), for_devices(dnorm.astype(BF16))], axis=1
    )
    sent, before, after = lax.optimization_barrier((sent, before, after))
    got = exchange(sent, "head")
    q, k, v, d = (got[:, n * piece : (n + 1) * piece].reshape(n_head * piece, dh) for n in range(4))
    rows = q.shape[0]
    causal = jnp.arange(rows)[:, None] >= jnp.arange(rows)[None, :]
    state = jnp.einsum("se,sf->ef", k, v, preferred_element_type=F32)

    def inner(q, k, v, d):
        scores = jnp.einsum("te,se->ts", q, k, preferred_element_type=F32)
        masked = jnp.where(causal, scores, 0.0).astype(BF16)
        return q, k, v, d, masked

    carried, (q, k, v, d, masked) = carry_states(state, (q, k, v, d), inner, False, before, groups)
    mixed = jnp.dot(q, carried, preferred_element_type=F32) + jnp.dot(masked, v, preferred_element_type=F32)
    inv = lax.rsqrt(jnp.mean(mixed * mixed, -1, keepdims=True) + 1e-05)
    normed = mixed * inv
    dnormed = d.astype(F32)
    dmixed = (inv * (dnormed - normed * jnp.mean(dnormed * normed, -1, keepdims=True))).astype(BF16)
    back_state = jnp.einsum("te,tf->ef", q, dmixed, preferred_element_type=F32)

    def inner_back(q, k, v, masked, dmixed, carried):
        within_v = jnp.einsum("ts,tf->sf", masked, dmixed, preferred_element_type=F32)
        across = jnp.einsum("tf,sf->ts", dmixed, v, preferred_element_type=F32)
        across = jnp.where(causal, across, 0.0).astype(BF16)
        grad_q = jnp.einsum("tf,ef->te", dmixed, carried, preferred_element_type=F32) + jnp.dot(
            across, k, preferred_element_type=F32
        )
        within_k = jnp.einsum("ts,te->se", across, q, preferred_element_type=F32)
        return k, v, grad_q.astype(BF16), within_k, within_v

    later, (k, v, grad_q, within_k, within_v) = carry_states(
        back_state, (q, k, v, masked, dmixed, carried), inner_back, True, after, groups
    )
    grad_k = jnp.einsum("sf,ef->se", v, later, preferred_element_type=F32) + within_k
    grad_v = jnp.dot(k, later, preferred_element_type=F32) + within_v
    grads = jnp.concatenate([g.astype(BF16).reshape(n_head, piece, dh) for g in (grad_q, grad_k, grad_v)], axis=1)
    back = exchange(grads, "head").reshape(xs, heads, cores, 3 * piece, dh).transpose(0, 2, 1, 3, 4)
    return tuple(back[:, :, :, n * piece : (n + 1) * piece].reshape(shape) for n in range(3))


def solution(mesh):
    placed = P(None, None, "ctx", "head", None, None)
    return jax.shard_map(
        local,
        mesh=mesh,
        in_specs=(placed,) * 5 + (P(),),
        out_specs=(placed,) * 3,
        check_vma=False,
    )
```

```python
import jax
import jax.numpy as jnp
from jax import lax
from jax.sharding import PartitionSpec as P

F32 = jnp.float32
BF16 = jnp.bfloat16


def exchange(x, axes, groups=None):
    return lax.all_to_all(x, axes, 0, 0, axis_index_groups=groups, tiled=True)


def to_pieces(state, n):
    rows, cols = state.shape
    tiles = -(-rows * cols // (8 * 128 * n)) * n
    high = tiles * 128 // cols * 8
    full = jnp.pad(state.astype(BF16), ((0, high - rows), (0, 0)))
    full = full.reshape(high // 8, 8, cols // 128, 128).transpose(0, 2, 1, 3)
    return full.reshape(n, tiles // n, 8, 128).transpose(0, 2, 1, 3).reshape(n, 8, tiles // n * 128)


def from_pieces(pieces, rows, cols):
    n, _, width = pieces.shape
    full = pieces.reshape(n, 8, width // 128, 128).transpose(0, 2, 1, 3)
    full = full.reshape(-1, cols // 128, 8, 128).transpose(0, 2, 1, 3).reshape(-1, cols)
    return full[:rows]


def carry_states(state, rest, meanwhile, reverse, wanted, groups):
    rows, cols = state.shape
    n_ctx = lax.axis_size("ctx")
    split = len(groups[0])
    at = jnp.arange(n_ctx)
    order = (at[:, None] < at[None, :] if reverse else at[:, None] > at[None, :]).astype(BF16)
    pieces, rest = lax.optimization_barrier((to_pieces(state, n_ctx), rest))
    pieces = exchange(pieces, "ctx")
    total = jnp.sum(pieces.astype(F32), 0)
    sent = jnp.broadcast_to(total.astype(BF16)[None], (split,) + total.shape)
    sent, rest = lax.optimization_barrier((sent, rest))
    totals = exchange(sent, "head", groups)
    totals, pieces = lax.optimization_barrier((totals, pieces))
    done = rest if meanwhile is None else meanwhile(*rest)
    inside = jnp.einsum("ab,brl->arl", order, pieces, preferred_element_type=F32)
    outside = jnp.sum(totals.astype(F32) * wanted[:, None, None], 0)
    back, done = lax.optimization_barrier(((inside + outside[None]).astype(BF16), done))
    back, done = lax.optimization_barrier((exchange(back, "ctx"), done))
    return from_pieces(back, rows, cols), done


def local(queries, keys, values, gates, out_grad, gains):
    split, heads, _, _, piece, dh = queries.shape
    shape = queries.shape
    n_head = lax.axis_size("head")
    xs, cores = n_head // (heads * 2), 2
    groups = [[((p // 2) * heads + h) * 2 + p % 2 for p in range(split)] for h in range(heads)]
    me = lax.axis_index("head")
    row = me // (heads * 2) * 2 + me % 2
    other = jnp.arange(split)
    before, after = ((other < row).astype(F32), (other > row).astype(F32))

    def for_devices(array):
        return array.reshape(xs, cores, heads, piece, dh).transpose(0, 2, 1, 3, 4).reshape(n_head, piece, dh)

    gate = gates.astype(F32)
    dnorm = out_grad.astype(F32) * gains[None, :, None, None, None, :] * jax.nn.silu(gate)
    sent = jnp.concatenate(
        [for_devices(queries), for_devices(keys), for_devices(values), for_devices(dnorm.astype(BF16))], axis=1
    )
    sent, before, after = lax.optimization_barrier((sent, before, after))
    got = exchange(sent, "head")
    q, k, v, d = (got[:, n * piece : (n + 1) * piece].reshape(n_head * piece, dh) for n in range(4))
    rows = q.shape[0]
    causal = jnp.arange(rows)[:, None] >= jnp.arange(rows)[None, :]
    state = jnp.einsum("se,sf->ef", k, v, preferred_element_type=F32)
    scores = jnp.einsum("te,se->ts", q, k, preferred_element_type=F32)
    masked = jnp.where(causal, scores, 0.0).astype(BF16)
    carried, (q, k, v, d, masked) = carry_states(state, (q, k, v, d, masked), None, False, before, groups)
    mixed = jnp.dot(q, carried, preferred_element_type=F32) + jnp.dot(masked, v, preferred_element_type=F32)
    inv = lax.rsqrt(jnp.mean(mixed * mixed, -1, keepdims=True) + 1e-05)
    normed = mixed * inv
    dnormed = d.astype(F32)
    dmixed = (inv * (dnormed - normed * jnp.mean(dnormed * normed, -1, keepdims=True))).astype(BF16)
    back_state = jnp.einsum("te,tf->ef", q, dmixed, preferred_element_type=F32)

    def inner_back(q, k, v, masked, dmixed, carried):
        within_v = jnp.einsum("ts,tf->sf", masked, dmixed, preferred_element_type=F32)
        across = jnp.einsum("tf,sf->ts", dmixed, v, preferred_element_type=F32)
        across = jnp.where(causal, across, 0.0).astype(BF16)
        grad_q = jnp.einsum("tf,ef->te", dmixed, carried, preferred_element_type=F32) + jnp.dot(
            across, k, preferred_element_type=F32
        )
        within_k = jnp.einsum("ts,te->se", across, q, preferred_element_type=F32)
        return k, v, grad_q.astype(BF16), within_k, within_v

    later, (k, v, grad_q, within_k, within_v) = carry_states(
        back_state, (q, k, v, masked, dmixed, carried), inner_back, True, after, groups
    )
    grad_k = jnp.einsum("sf,ef->se", v, later, preferred_element_type=F32) + within_k
    grad_v = jnp.dot(k, later, preferred_element_type=F32) + within_v
    grads = jnp.concatenate([g.astype(BF16).reshape(n_head, piece, dh) for g in (grad_q, grad_k, grad_v)], axis=1)
    grads = lax.optimization_barrier(grads)
    half = dh // 2
    back = exchange(jnp.concatenate([grads[:, :, :half], grads[:, :, half:]], axis=1), "head")
    back = lax.optimization_barrier(jnp.concatenate([back[:, : 3 * piece], back[:, 3 * piece :]], axis=-1))
    back = back.reshape(xs, heads, cores, 3 * piece, dh).transpose(0, 2, 3, 1, 4)
    back = lax.optimization_barrier(back.reshape(split, 3 * piece, heads, dh))
    back = back.transpose(0, 2, 1, 3)
    return tuple(back[:, :, n * piece : (n + 1) * piece].reshape(shape) for n in range(3))


def solution(mesh):
    placed = P(None, None, "ctx", "head", None, None)
    return jax.shard_map(
        local,
        mesh=mesh,
        in_specs=(placed,) * 5 + (P(),),
        out_specs=(placed,) * 3,
        check_vma=False,
    )
```

```python
import jax
import jax.numpy as jnp
from jax import lax
from jax.sharding import PartitionSpec as P

F32 = jnp.float32
BF16 = jnp.bfloat16


def exchange(x, axes, groups=None):
    return lax.all_to_all(x, axes, 0, 0, axis_index_groups=groups, tiled=True)


def to_pieces(state, n):
    rows, cols = state.shape
    tiles = -(-rows * cols // (8 * 128 * n)) * n
    high = tiles * 128 // cols * 8
    full = jnp.pad(state.astype(BF16), ((0, high - rows), (0, 0)))
    full = full.reshape(high // 8, 8, cols // 128, 128).transpose(0, 2, 1, 3)
    return full.reshape(n, tiles // n, 8, 128).transpose(0, 2, 1, 3).reshape(n, 8, tiles // n * 128)


def from_pieces(pieces, rows, cols):
    n, _, width = pieces.shape
    full = pieces.reshape(n, 8, width // 128, 128).transpose(0, 2, 1, 3)
    full = full.reshape(-1, cols // 128, 8, 128).transpose(0, 2, 1, 3).reshape(-1, cols)
    return full[:rows]


def carry_states(state, rest, meanwhile, reverse, wanted, groups):
    rows, cols = state.shape
    n_ctx = lax.axis_size("ctx")
    split = len(groups[0])
    at = jnp.arange(n_ctx)
    order = (at[:, None] < at[None, :] if reverse else at[:, None] > at[None, :]).astype(BF16)
    pieces, rest = lax.optimization_barrier((to_pieces(state, n_ctx), rest))
    pieces = exchange(pieces, "ctx")
    total = lax.optimization_barrier(jnp.sum(pieces.astype(F32), 0))
    sent = jnp.broadcast_to(total.astype(BF16)[None], (split,) + total.shape)
    sent, rest = lax.optimization_barrier((sent, rest))
    totals = exchange(sent, "head", groups)
    totals, pieces = lax.optimization_barrier((totals, pieces))
    done = rest if meanwhile is None else meanwhile(*rest)
    inside = jnp.einsum("ab,brl->arl", order, pieces, preferred_element_type=F32)
    outside = jnp.sum(totals.astype(F32) * wanted[:, None, None], 0)
    back, done = lax.optimization_barrier(((inside + outside[None]).astype(BF16), done))
    back, done = lax.optimization_barrier((exchange(back, "ctx"), done))
    return from_pieces(back, rows, cols), done


def local(queries, keys, values, gates, out_grad, gains):
    split, heads, _, _, piece, dh = queries.shape
    shape = queries.shape
    n_head = lax.axis_size("head")
    xs, cores = n_head // (heads * 2), 2
    groups = [[((p // 2) * heads + h) * 2 + p % 2 for p in range(split)] for h in range(heads)]
    me = lax.axis_index("head")
    row = me // (heads * 2) * 2 + me % 2
    other = jnp.arange(split)
    before, after = ((other < row).astype(F32), (other > row).astype(F32))

    def by_token(array):
        return array.reshape(split, heads, piece, dh).transpose(0, 2, 1, 3)

    gate = by_token(gates).astype(F32)
    dnorm = by_token(out_grad).astype(F32) * gains[None, None] * jax.nn.silu(gate)
    sent = jnp.concatenate([by_token(queries), by_token(keys), by_token(values), dnorm.astype(BF16)], axis=1)
    sent = lax.optimization_barrier(sent).reshape(xs, cores, 4 * piece, heads, dh)
    sent = sent.transpose(0, 3, 1, 2, 4).reshape(n_head, 4 * piece, dh)
    sent, before, after = lax.optimization_barrier((sent, before, after))
    got = exchange(sent, "head")
    q, k, v, d = (got[:, n * piece : (n + 1) * piece].reshape(n_head * piece, dh) for n in range(4))
    rows = q.shape[0]
    causal = jnp.arange(rows)[:, None] >= jnp.arange(rows)[None, :]
    state = jnp.einsum("se,sf->ef", k, v, preferred_element_type=F32)
    scores = jnp.einsum("te,se->ts", q, k, preferred_element_type=F32)
    masked = jnp.where(causal, scores, 0.0).astype(BF16)
    carried, (q, k, v, d, masked) = carry_states(state, (q, k, v, d, masked), None, False, before, groups)
    mixed = jnp.dot(q, carried, preferred_element_type=F32) + jnp.dot(masked, v, preferred_element_type=F32)
    inv = lax.rsqrt(jnp.mean(mixed * mixed, -1, keepdims=True) + 1e-05)
    normed = mixed * inv
    dnormed = d.astype(F32)
    dmixed = (inv * (dnormed - normed * jnp.mean(dnormed * normed, -1, keepdims=True))).astype(BF16)
    back_state = jnp.einsum("te,tf->ef", q, dmixed, preferred_element_type=F32)

    def inner_back(q, k, v, masked, dmixed, carried):
        within_v = jnp.einsum("ts,tf->sf", masked, dmixed, preferred_element_type=F32)
        across = jnp.einsum("tf,sf->ts", dmixed, v, preferred_element_type=F32)
        across = jnp.where(causal, across, 0.0).astype(BF16)
        grad_q = jnp.einsum("tf,ef->te", dmixed, carried, preferred_element_type=F32) + jnp.dot(
            across, k, preferred_element_type=F32
        )
        within_k = jnp.einsum("ts,te->se", across, q, preferred_element_type=F32)
        return k, v, grad_q.astype(BF16), within_k, within_v

    later, (k, v, grad_q, within_k, within_v) = carry_states(
        back_state, (q, k, v, masked, dmixed, carried), inner_back, True, after, groups
    )
    grad_k = jnp.einsum("sf,ef->se", v, later, preferred_element_type=F32) + within_k
    grad_v = jnp.dot(k, later, preferred_element_type=F32) + within_v
    grads = jnp.concatenate([g.astype(BF16).reshape(n_head, piece, dh) for g in (grad_q, grad_k, grad_v)], axis=1)
    grads = lax.optimization_barrier(grads)
    half = dh // 2
    back = exchange(jnp.concatenate([grads[:, :, :half], grads[:, :, half:]], axis=1), "head")
    back = lax.optimization_barrier(jnp.concatenate([back[:, : 3 * piece], back[:, 3 * piece :]], axis=-1))
    back = back.reshape(xs, heads, cores, 3 * piece, dh).transpose(0, 2, 3, 1, 4)
    back = lax.optimization_barrier(back.reshape(split, 3 * piece, heads, dh))
    back = back.transpose(0, 2, 1, 3)
    return tuple(back[:, :, n * piece : (n + 1) * piece].reshape(shape) for n in range(3))


def solution(mesh):
    placed = P(None, None, "ctx", "head", None, None)
    return jax.shard_map(
        local,
        mesh=mesh,
        in_specs=(placed,) * 5 + (P(),),
        out_specs=(placed,) * 3,
        check_vma=False,
    )
```

```python
import jax
import jax.numpy as jnp
from jax import lax
from jax.sharding import PartitionSpec as P

F32 = jnp.float32
BF16 = jnp.bfloat16


def exchange(x, axes, groups=None):
    return lax.all_to_all(x, axes, 0, 0, axis_index_groups=groups, tiled=True)


def to_pieces(state, n):
    rows, cols = state.shape
    tiles = -(-rows * cols // (8 * 128 * n)) * n
    high = tiles * 128 // cols * 8
    full = jnp.pad(state.astype(BF16), ((0, high - rows), (0, 0)))
    full = full.reshape(high // 8, 8, cols // 128, 128).transpose(0, 2, 1, 3)
    return full.reshape(n, tiles // n, 8, 128).transpose(0, 2, 1, 3).reshape(n, 8, tiles // n * 128)


def from_pieces(pieces, rows, cols):
    n, _, width = pieces.shape
    full = pieces.reshape(n, 8, width // 128, 128).transpose(0, 2, 1, 3)
    full = full.reshape(-1, cols // 128, 8, 128).transpose(0, 2, 1, 3).reshape(-1, cols)
    return full[:rows]


def carry_states(state, rest, meanwhile, reverse, wanted, groups):
    rows, cols = state.shape
    n_ctx = lax.axis_size("ctx")
    split = len(groups[0])
    at = jnp.arange(n_ctx)
    order = (at[:, None] < at[None, :] if reverse else at[:, None] > at[None, :]).astype(BF16)
    pieces, rest = lax.optimization_barrier((to_pieces(state, n_ctx), rest))
    pieces = exchange(pieces, "ctx")
    total = lax.optimization_barrier(jnp.sum(pieces.astype(F32), 0))
    sent = jnp.broadcast_to(total.astype(BF16)[None], (split,) + total.shape)
    sent, rest = lax.optimization_barrier((sent, rest))
    totals = exchange(sent, "head", groups)
    totals, pieces = lax.optimization_barrier((totals, pieces))
    done = rest if meanwhile is None else meanwhile(*rest)
    inside = jnp.einsum("ab,brl->arl", order, pieces, preferred_element_type=F32)
    outside = jnp.sum(totals.astype(F32) * wanted[:, None, None], 0)
    back, done = lax.optimization_barrier(((inside + outside[None]).astype(BF16), done))
    back, done = lax.optimization_barrier((exchange(back, "ctx"), done))
    return from_pieces(back, rows, cols), done


def local(queries, keys, values, gates, out_grad, gains):
    split, heads, _, _, piece, dh = queries.shape
    shape = queries.shape
    n_head = lax.axis_size("head")
    xs, cores = n_head // (heads * 2), 2
    groups = [[((p // 2) * heads + h) * 2 + p % 2 for p in range(split)] for h in range(heads)]
    me = lax.axis_index("head")
    row = me // (heads * 2) * 2 + me % 2
    other = jnp.arange(split)
    before, after = ((other < row).astype(F32), (other > row).astype(F32))

    def by_token(array):
        return array.reshape(split, heads, piece, dh).transpose(0, 2, 1, 3)

    gate = by_token(gates).astype(F32)
    dnorm = by_token(out_grad).astype(F32) * gains[None, None] * jax.nn.silu(gate)
    sent = jnp.concatenate([by_token(queries), by_token(keys), by_token(values), dnorm.astype(BF16)], axis=1)
    sent = lax.optimization_barrier(sent).reshape(xs, cores, 4 * piece, heads, dh)
    sent = sent.transpose(0, 3, 1, 2, 4).reshape(n_head, 4 * piece, dh)
    sent, before, after = lax.optimization_barrier((sent, before, after))
    got = exchange(sent, "head")
    q, k, v, d = (got[:, n * piece : (n + 1) * piece].reshape(n_head * piece, dh) for n in range(4))
    rows = q.shape[0]
    causal = jnp.arange(rows)[:, None] >= jnp.arange(rows)[None, :]
    state = jnp.einsum("se,sf->ef", k, v, preferred_element_type=F32)
    scores = jnp.einsum("te,se->ts", q, k, preferred_element_type=F32)
    masked = jnp.where(causal, scores, 0.0).astype(BF16)
    carried, (q, k, v, d, masked) = carry_states(state, (q, k, v, d, masked), None, False, before, groups)
    mixed = jnp.dot(q, carried, preferred_element_type=F32) + jnp.dot(masked, v, preferred_element_type=F32)
    inv = lax.rsqrt(jnp.mean(mixed * mixed, -1, keepdims=True) + 1e-05)
    normed = mixed * inv
    dnormed = d.astype(F32)
    dmixed = (inv * (dnormed - normed * jnp.mean(dnormed * normed, -1, keepdims=True))).astype(BF16)
    back_state = jnp.einsum("te,tf->ef", q, dmixed, preferred_element_type=F32)

    def inner_back(q, k, v, masked, dmixed, carried):
        within_v = jnp.einsum("ts,tf->sf", masked, dmixed, preferred_element_type=F32)
        across = jnp.einsum("tf,sf->ts", dmixed, v, preferred_element_type=F32)
        across = jnp.where(causal, across, 0.0).astype(BF16)
        grad_q = jnp.einsum("tf,ef->te", dmixed, carried, preferred_element_type=F32) + jnp.dot(
            across, k, preferred_element_type=F32
        )
        within_k = jnp.einsum("ts,te->se", across, q, preferred_element_type=F32)
        return k, v, grad_q.astype(BF16), within_k.astype(BF16), within_v.astype(BF16)

    later, (k, v, grad_q, within_k, within_v) = carry_states(
        back_state, (q, k, v, masked, dmixed, carried), inner_back, True, after, groups
    )
    grad_k = jnp.einsum("sf,ef->se", v, later, preferred_element_type=F32) + within_k
    grad_v = jnp.dot(k, later, preferred_element_type=F32) + within_v
    grads = jnp.concatenate([g.astype(BF16).reshape(n_head, piece, dh) for g in (grad_q, grad_k, grad_v)], axis=1)
    grads = lax.optimization_barrier(grads)
    half = dh // 2
    back = exchange(jnp.concatenate([grads[:, :, :half], grads[:, :, half:]], axis=1), "head")
    back = lax.optimization_barrier(jnp.concatenate([back[:, : 3 * piece], back[:, 3 * piece :]], axis=-1))
    back = back.reshape(xs, heads, cores, 3 * piece, dh).transpose(0, 2, 3, 1, 4)
    back = lax.optimization_barrier(back.reshape(split, 3 * piece, heads, dh))
    back = back.transpose(0, 2, 1, 3)
    return tuple(back[:, :, n * piece : (n + 1) * piece].reshape(shape) for n in range(3))


def solution(mesh):
    placed = P(None, None, "ctx", "head", None, None)
    return jax.shard_map(
        local,
        mesh=mesh,
        in_specs=(placed,) * 5 + (P(),),
        out_specs=(placed,) * 3,
        check_vma=False,
    )
```
